256 devices in a mesh: src: 16 (over x, y_lo, core), rcv: 16 (over y_hi, z).
Axes of the slice: x: 4, y: 4 (y_hi: 2, y_lo: 2; y = y_hi * 2 + y_lo), z: 8, core: 2. Of those that a mesh axis runs over, the one named last changes fastest.
Arguments:
- data: bfloat16 [2, 512, 512, 256], P(None, 'src', 'rcv'), as said below
- panel_index: int32 [2, 32], replicated, may hold values from 0 to 511, as said below
- panel_weight: float32 [2, 32], replicated, may hold values from 0.25 to 1.75
- band_index: int32 [256], replicated, may hold values from 1 to 512, as said below
Outputs:
- predicted: bfloat16 [512, 512, 1024], P('src', 'rcv')
The draws below stay inside these ranges and needn't reach their ends.
Inputs may be any that keep to these rules, and one draw needn't show every extreme that they name: data is unchanged when the source and receiver indices are exchanged (reciprocity). `panel_index`: each row holds the 32 traces of one aligned group of 32 trace numbers, each once, in some order; one row holds the first group and another the last. `band_index`: distinct bins.
All inputs are finite; a program needn't handle non-finite values.
Results may differ from the reference program's by a relative error of at most 0.0062.
Values may be sent and summed in bfloat16 or wider, within the bound.
A program may use at most 128 MiB of HBM per device.

```python
import math
import jax
import jax.numpy as jnp
from jax import lax

NF = 256
NT = 1024
PANEL = 32
STEPS = 2
NTR = 512


def draw_data(key, part):
    key = jax.random.fold_in(key, 11)
    full_shape = (2, NTR, NTR, NF)
    base_draw = jax.random.normal(key, full_shape, jnp.float32)
    mirrored = (base_draw + jnp.swapaxes(base_draw, 1, 2)) * 0.70710678
    return mirrored.astype(jnp.bfloat16)


def draw_panel_index(key, part):
    key = jax.random.fold_in(key, 23)
    key_group, key_order, key_flip = jax.random.split(key, 3)
    last_group = NTR // PANEL - 1
    groups = jax.random.randint(key_group, (STEPS,), 0, NTR // PANEL, dtype=jnp.int32)
    flip = jax.random.randint(key_flip, (), 0, 2, dtype=jnp.int32)
    groups = groups.at[0].set(flip * last_group)
    groups = groups.at[STEPS - 1].set((1 - flip) * last_group)
    order_keys = jax.random.split(key_order, STEPS)
    orders = jax.vmap(lambda single: jax.random.permutation(single, PANEL))(order_keys)
    return (groups[:, None] * PANEL + orders).astype(jnp.int32)


def draw_band_index(key, part):
    key = jax.random.fold_in(key, 37)
    key_inner, key_shuffle = jax.random.split(key)
    inner = jax.random.permutation(key_inner, NT // 2 - 2)[:NF - 2].astype(jnp.int32) + 2
    values = jnp.concatenate([jnp.array([1, NT // 2], dtype=jnp.int32), inner])
    return jax.random.permutation(key_shuffle, values).astype(jnp.int32)


def setup_inputs(seed: int = 0) -> dict:
    key_list = jax.random.split(jax.random.key(seed), 5)
    data = draw_data(jax.random.fold_in(key_list[4], 71), 0)
    panel_index = draw_panel_index(jax.random.fold_in(key_list[4], 71), 0)
    panel_weight = jnp.clip(jax.random.uniform(key_list[2], (STEPS, PANEL), jnp.float32, 0.25, 1.75), 0.25, 1.75)
    band_index = draw_band_index(jax.random.fold_in(key_list[4], 71), 0)
    return dict(data=data, panel_index=panel_index, panel_weight=panel_weight, band_index=band_index)


def phase_table(band_index):
    sample_times = jnp.arange(NT, dtype=jnp.int32)
    phase_turns = band_index.astype(jnp.int32)[:, None] * sample_times[None, :] % NT
    phase_angle = phase_turns.astype(jnp.float32) * (2.0 * math.pi / NT)
    cos_table = jnp.cos(phase_angle).astype(jnp.bfloat16)
    sin_table = jnp.sin(phase_angle).astype(jnp.bfloat16)
    return jnp.concatenate([cos_table, -sin_table], axis=0)

def reference(data, panel_index, panel_weight, band_index):
    wave_table = phase_table(band_index)
    norm_scale = 1.0 / math.sqrt(2.0 * STEPS * PANEL * NF)
    flat_index = panel_index.reshape(-1).astype(jnp.int32)
    columns = jnp.take(data, flat_index, axis=2)
    weighted = (columns.astype(jnp.float32) * panel_weight.reshape(-1)[None, None, :, None]).astype(jnp.bfloat16)
    right_panel = jnp.take(data, flat_index, axis=1).astype(jnp.float32)

    def one_block(row_start):
        left_block = lax.dynamic_slice_in_dim(weighted, row_start, PANEL, 1).astype(jnp.float32)
        spec_re = jnp.einsum('spf,prf->srf', left_block[0], right_panel[0]) - jnp.einsum('spf,prf->srf', left_block[1], right_panel[1])
        spec_im = jnp.einsum('spf,prf->srf', left_block[0], right_panel[1]) + jnp.einsum('spf,prf->srf', left_block[1], right_panel[0])
        stacked = jnp.concatenate([spec_re, spec_im], axis=2).reshape(PANEL * NTR, 2 * NF).astype(jnp.bfloat16)
        traces_time = jnp.dot(stacked, wave_table, preferred_element_type=jnp.float32)
        return (-norm_scale * traces_time).reshape(PANEL, NTR, NT).astype(jnp.bfloat16)
    starts = jnp.arange(NTR // PANEL, dtype=jnp.int32) * PANEL
    blocks = lax.map(one_block, starts)
    return blocks.reshape(NTR, NTR, NT)
```

```python
import functools
import math

import jax
import jax.numpy as jnp
from jax import lax
from jax.experimental import pallas as pl
from jax.experimental.pallas import tpu as pltpu
from jax.sharding import PartitionSpec as P

NF = 256
NT = 1024
PANEL = 32
STEPS = 2
BLK = 32
LANES = 128
HALF = 64
CH = 4
NCH = 8
SLOPE = 3
LAG = 3
MESH = pl.DeviceIdType.MESH


def device(x, lo, core, h, z):
    return (x * 4 + lo * 2 + core, h * 8 + z)


def here():
    src = lax.axis_index("src")
    rcv = lax.axis_index("rcv")
    return src // 4, (src // 2) % 2, src % 2, rcv // 8, rcv % 8


def after(depth):
    return (depth * SLOPE) // 2


def gather_kernel(
    data, weight, band, z_out, table,
    turned, left, right, spec_out, spec_in,
    l_send, l_recv, r_send, r_recv, s_send, s_recv,
):
    x, lo, core, h, z = here()
    other = 1 - h

    barrier = pltpu.get_barrier_semaphore()
    neighbours = [
        device(x, lo, core, h, (z + 1) % 8),
        device(x, lo, core, h, (z + 7) % 8),
        device(x, lo, core, other, z),
        device(x, 1 - lo, core, h, z),
        device((x + 1) % 4, lo, core, h, z),
        device((x + 3) % 4, lo, core, h, z),
        device(x, lo, 1 - core, h, z),
    ]
    for one in neighbours:
        pl.semaphore_signal(barrier, inc=1, device_id=one, device_id_type=MESH)

    seen = [(x, lo, core, h, z), (3 - x, 1 - lo, 1 - core, 1 - h, 7 - z)]
    step = [1, -1]

    for g in range(2):
        xm, lm, cm, hm, zm = seen[g]

        @pl.when((hm == 0) & (zm == 0))
        def _():
            scale = weight[g]

            @pl.loop(0, BLK, unroll=2)
            def _(s):
                rows = jnp.concatenate(
                    [
                        (
                            data[c, s, :, fh * LANES : (fh + 1) * LANES].astype(
                                jnp.float32
                            )
                            * scale
                        )
                        .astype(jnp.bfloat16)
                        .astype(jnp.float32)
                        for fh in range(2)
                        for c in range(2)
                    ],
                    axis=0,
                )
                turned[pl.ds(s, LANES, stride=BLK), :] = rows.T

            @pl.loop(0, LANES, unroll=4)
            def _(f):
                left[g, f] = turned[pl.ds(f * BLK, BLK), :].astype(jnp.bfloat16)

        @pl.when((xm == 0) & (lm == 0) & (cm == 0))
        def _():
            @pl.loop(0, BLK, unroll=2)
            def _(q):
                rows = jnp.concatenate(
                    [
                        data[c, q, :, fh * LANES : (fh + 1) * LANES].astype(jnp.float32)
                        for c in range(2)
                        for fh in range(2)
                    ],
                    axis=0,
                )
                turned[pl.ds(q, LANES, stride=BLK), :] = rows.T

            @pl.loop(0, LANES, unroll=4)
            def _(f):
                right[g, 0, f // HALF, (f // BLK) % 2, f % BLK] = turned[
                    pl.ds(f * BLK, BLK), :
                ].astype(jnp.bfloat16)

    pl.semaphore_wait(barrier, len(neighbours))

    def left_copy(g, d, k, row, slot, target):
        start = row * HALF + d * BLK + k * CH
        ref = left.at[g, pl.ds(start, CH)]
        return pltpu.make_async_remote_copy(
            src_ref=ref, dst_ref=ref,
            send_sem=l_send.at[g, d, k, slot], recv_sem=l_recv.at[g, d, k],
            device_id=target, device_id_type=MESH,
        )

    def right_copy(g, rel, k, row, slot, target, cross=False):
        return pltpu.make_async_remote_copy(
            src_ref=right.at[g, 0 if cross else rel, row, :, pl.ds(k * CH, CH)],
            dst_ref=right.at[g, rel, row, :, pl.ds(k * CH, CH)],
            send_sem=r_send.at[g, rel, k, slot], recv_sem=r_recv.at[g, rel, k],
            device_id=target, device_id_type=MESH,
        )

    def spec_copy(d, k):
        return pltpu.make_async_remote_copy(
            src_ref=spec_out.at[d, pl.ds(k * CH, CH)],
            dst_ref=spec_in.at[d, pl.ds(k * CH, CH)],
            send_sem=s_send.at[d, k], recv_sem=s_recv.at[d, k],
            device_id=device(x, lo, core, other, z), device_id_type=MESH,
        )

    def left_plan(g, d):
        _, _, _, hm, zm = seen[g]
        pos = zm if d == 0 else (8 - zm) % 8
        along = step[g] if d == 0 else -step[g]
        onward = device(x, lo, core, h, (z + along + 8) % 8)
        return pos, pos + hm, (pos == 0) & (hm == 0), onward

    def right_plan(g, rel):
        xm, lm, cm, _, _ = seen[g]
        first = jnp.where(xm == 3, 1, xm)
        root = (xm == 0) & (lm == 0) & (cm == 0)
        return xm, lm, cm, root, rel + lm + first + cm

    def right_sends(g, rel):
        xm, lm, cm, root, _ = right_plan(g, rel)
        up, down = (x + step[g] + 4) % 4, (x - step[g] + 4) % 4
        return [
            (cm == 0, device(x, lo, 1 - core, h, z)),
            ((cm == 0) & (xm == 0) & (lm == 0), device(x, 1 - lo, core, h, z)),
            ((cm == 0) & (xm <= 1), device(up, lo, core, h, z)),
            ((cm == 0) & (xm == 0), device(down, lo, core, h, z)),
        ]

    partner = device(x, lo, core, other, z)
    reach = []
    reach_other = []
    for d in range(2):
        mine = theirs = jnp.int32(0)
        for g in range(2):
            pos, depth, _, _ = left_plan(g, d)
            mine = jnp.maximum(mine, depth)
            theirs = jnp.maximum(theirs, pos + (1 - seen[g][3]))
            right_depth = right_plan(g, 1)[4]
            mine = jnp.maximum(mine, right_depth)
            theirs = jnp.maximum(theirs, right_depth)
        reach.append(after(mine))
        reach_other.append(after(jnp.maximum(mine, theirs)) + LAG)

    lane = lax.broadcasted_iota(jnp.int32, (BLK, LANES), 1)
    in_half = [(lane // BLK) % 2 == fh for fh in range(2)]
    keep = [jnp.where(m, 1.0, 0.0).astype(jnp.bfloat16) for m in in_half]
    sign = [
        jnp.where(m, jnp.where(lane < HALF, -1.0, 1.0), 0.0).astype(jnp.bfloat16)
        for m in in_half
    ]

    def spectra(d, k):
        @pl.loop(0, CH, unroll=True)
        def _(i):
            f = h * HALF + d * BLK + k * CH + i
            rows = jnp.concatenate([left[0, f], left[1, f]], axis=1)
            columns = []
            for rel in range(2):
                parts = []
                for g in range(2):
                    held = right[g, rel, h, d, k * CH + i]
                    swapped = jnp.concatenate([held[:, HALF:], held[:, :HALF]], axis=1)
                    for fh in range(2):
                        parts += [held * keep[fh], swapped * sign[fh]]
                columns.append(jnp.concatenate(parts, axis=0))
            product = jnp.dot(
                rows,
                jnp.concatenate(columns, axis=1),
                preferred_element_type=jnp.float32,
            )
            z_out[pl.ds(f, BLK, stride=LANES), :] = product[:, :LANES]
            spec_out[d, k * CH + i] = product[:, LANES:].astype(jnp.bfloat16)

        spec_copy(d, k).start()

    def take_in(d, k):
        spec_copy(d, k).wait_recv()

        @pl.loop(0, CH, unroll=True)
        def _(i):
            f = other * HALF + d * BLK + k * CH + i
            z_out[pl.ds(f, BLK, stride=LANES), :] = spec_in[d, k * CH + i].astype(
                jnp.float32
            )

    def within(k):
        return (k >= 0) & (k < NCH)

    slots = NCH + after(8) + LAG

    @pl.loop(0, slots)
    def _(t):
        for g in range(2):
            for d in range(2):
                pos, depth, source, onward = left_plan(g, d)
                k = t - after(depth)

                @pl.when(within(k))
                def _():
                    own = left_copy(g, d, k, h, 0, onward)

                    @pl.when(jnp.logical_not(source))
                    def _():
                        own.wait_recv()

                    @pl.when(pos < 7)
                    def _():
                        own.start()

                    @pl.when(source)
                    def _():
                        left_copy(g, d, k, other, 1, partner).start()

            for rel in range(2):
                xm, lm, cm, root, depth = right_plan(g, rel)
                k = t - after(depth)

                @pl.when(within(k))
                def _():
                    awaited = jnp.logical_not(root) if rel == 0 else root | True

                    @pl.when(awaited)
                    def _():
                        right_copy(g, rel, k, h, 0, partner).wait_recv()

                    for slot, (sends, target) in enumerate(right_sends(g, rel)):

                        @pl.when(sends)
                        def _():
                            right_copy(g, rel, k, h, slot, target).start()

                    if rel == 0:

                        @pl.when(root)
                        def _():
                            right_copy(g, 1, k, other, 4, partner, True).start()

        for d in range(2):
            k = t - reach[d]

            @pl.when(within(k))
            def _():
                spectra(d, k)

            k_in = t - reach_other[d]

            @pl.when(within(k_in))
            def _():
                take_in(d, k_in)

        if True:

            @pl.when(t == 0)
            def _():
                turns = jnp.float32(2.0 * math.pi / NT)
                bins = band[...]
                sample = lax.broadcasted_iota(jnp.int32, (NF, LANES), 1)
                fine = ((bins * sample) & (NT - 1)).astype(jnp.float32) * turns
                cos_fine, sin_fine = jnp.cos(fine), jnp.sin(fine)
                for block in range(NT // LANES):
                    coarse = ((bins * (block * LANES)) & (NT - 1)).astype(
                        jnp.float32
                    ) * turns
                    cos_coarse, sin_coarse = jnp.cos(coarse), jnp.sin(coarse)
                    at = slice(block * LANES, (block + 1) * LANES)
                    table[:NF, at] = (
                        cos_coarse * cos_fine - sin_coarse * sin_fine
                    ).astype(jnp.bfloat16)
                    table[NF:, at] = (
                        -(sin_coarse * cos_fine + cos_coarse * sin_fine)
                    ).astype(jnp.bfloat16)

    @pl.loop(0, NCH)
    def _(k):
        for d in range(2):
            spec_copy(d, k).wait_send()
            for g in range(2):
                pos, _, source, onward = left_plan(g, d)

                @pl.when(pos < 7)
                def _():
                    left_copy(g, d, k, h, 0, onward).wait_send()

                @pl.when(source)
                def _():
                    left_copy(g, d, k, other, 1, partner).wait_send()

        for g in range(2):
            for rel in range(2):
                for slot, (sends, target) in enumerate(right_sends(g, rel)):

                    @pl.when(sends)
                    def _():
                        right_copy(g, rel, k, h, slot, target).wait_send()

            @pl.when(right_plan(g, 0)[3])
            def _():
                right_copy(g, 1, k, other, 4, partner, True).wait_send()


def gathered_spectra(data, weight, band):
    vmem = pl.BlockSpec(memory_space=pltpu.VMEM)
    dma = pltpu.SemaphoreType.DMA
    bf16 = jnp.bfloat16
    return pl.pallas_call(
        gather_kernel,
        out_shape=(
            jax.ShapeDtypeStruct((BLK * LANES, LANES), jnp.float32),
            jax.ShapeDtypeStruct((2 * NF, NT), bf16),
        ),
        in_specs=[vmem] * 3,
        out_specs=(vmem, vmem),
        scratch_shapes=[
            pltpu.VMEM((LANES * BLK, LANES), jnp.float32),
            pltpu.VMEM((2, LANES, BLK, LANES), bf16),
            pltpu.VMEM((2, 2, 2, 2, BLK, BLK, LANES), bf16),
            pltpu.VMEM((2, BLK, BLK, LANES), bf16),
            pltpu.VMEM((2, BLK, BLK, LANES), bf16),
            dma((2, 2, NCH, 2)),
            dma((2, 2, NCH)),
            dma((2, 2, NCH, 5)),
            dma((2, 2, NCH)),
            dma((2, NCH)),
            dma((2, NCH)),
        ],
        compiler_params=pltpu.CompilerParams(
            collective_id=0, has_side_effects=True, vmem_limit_bytes=40 * 2**20
        ),
        cost_estimate=pl.CostEstimate(
            flops=2 * HALF * BLK * 256 * 256,
            bytes_accessed=6 * 2**20,
            transcendentals=2 * NF * LANES,
        ),
        name="gathered_spectra",
    )(data, weight, band)


ROWS_AT_ONCE = 8


def to_time_kernel(scale, z_ref, table, out):
    rows = []
    for s in range(ROWS_AT_ONCE):
        turned = z_ref[s * LANES : (s + 1) * LANES, :].T.astype(jnp.bfloat16)
        rows.append(
            jnp.concatenate(
                [turned[j * BLK : (j + 1) * BLK, :] for j in range(4)], axis=1
            )
        )
    product = jnp.dot(
        jnp.concatenate(rows, axis=0), table[...], preferred_element_type=jnp.float32
    )
    out[...] = (product * scale).astype(jnp.bfloat16).reshape(ROWS_AT_ONCE, BLK, NT)


def to_time(z, table, scale):
    steps = BLK // ROWS_AT_ONCE
    return pl.pallas_call(
        functools.partial(to_time_kernel, scale),
        out_shape=jax.ShapeDtypeStruct((BLK, BLK, NT), jnp.bfloat16),
        grid=(steps,),
        in_specs=[
            pl.BlockSpec((ROWS_AT_ONCE * LANES, LANES), lambda i: (i, 0)),
            pl.BlockSpec((2 * NF, NT), lambda i: (0, 0)),
        ],
        out_specs=pl.BlockSpec((ROWS_AT_ONCE, BLK, NT), lambda i: (i, 0, 0)),
        compiler_params=pltpu.CompilerParams(vmem_limit_bytes=40 * 2**20),
        cost_estimate=pl.CostEstimate(
            flops=2 * 1024 * 512 * 1024, bytes_accessed=5 * 2**20, transcendentals=0
        ),
        name="to_time",
    )(z, table)


def body(data, panel_index, panel_weight, band_index):
    group_start = jnp.array([0, 512 - PANEL], jnp.int32)
    traces = group_start[:, None] + jnp.arange(PANEL, dtype=jnp.int32)[None, :]
    found = traces[:, :, None] == panel_index.reshape(-1)[None, None, :]
    weight = jnp.sum(
        jnp.where(found, panel_weight.reshape(-1)[None, None, :], 0.0), axis=2
    )
    weight = jnp.broadcast_to(weight[:, :, None], (2, PANEL, LANES))
    z, table = gathered_spectra(data, weight, band_index.reshape(NF, 1))
    norm_scale = 1.0 / math.sqrt(2.0 * STEPS * PANEL * NF)
    return to_time(z, table, -norm_scale)


def solution(mesh):
    placed = (P(None, "src", "rcv", None), P(), P(), P())
    return jax.shard_map(
        body, mesh=mesh, in_specs=placed, out_specs=P("src", "rcv", None), check_vma=False
    )
```

```python
import functools
import math

import jax
import jax.numpy as jnp
from jax import lax
from jax.experimental import pallas as pl
from jax.experimental.pallas import tpu as pltpu
from jax.sharding import PartitionSpec as P

NF = 256
NT = 1024
PANEL = 32
STEPS = 2
BLK = 32
LANES = 128
HALF = 64
CH = 4
MESH = pl.DeviceIdType.MESH


def device(x, lo, core, h, z):
    return (x * 4 + lo * 2 + core, h * 8 + z)


def here():
    src = lax.axis_index("src")
    rcv = lax.axis_index("rcv")
    return src // 4, (src // 2) % 2, src % 2, rcv // 8, rcv % 8


def gather_kernel(
    data_hbm, index_hbm, weight_hbm, band_hbm, z_out, table,
    data, panel_index, panel_weight, band, turned, left, right, spec_out, spec_in,
    data_sem, small_sem, l_recv, l_first, l_send, r_recv, r_first, r_send, r_side,
    s_send, s_recv,
):
    x, lo, core, h, z = here()
    other = 1 - h
    partner = device(x, lo, core, other, z)
    sibling = device(x, lo, 1 - core, h, z)
    l_source = [(h == g) & (z == 7 * g) for g in range(2)]
    root = (x == 3 * core) & (lo == core)
    any_source = l_source[0] | l_source[1]

    def z_off(dz):
        return (z + dz + 8) % 8

    def x_off(dx):
        return (x + dx) % 4

    @pl.when(any_source | root)
    def _():
        pltpu.make_async_copy(data_hbm, data, data_sem).start()

    small = [
        pltpu.make_async_copy(src, dst, small_sem.at[i])
        for i, (src, dst) in enumerate(
            ((index_hbm, panel_index), (weight_hbm, panel_weight), (band_hbm, band))
        )
    ]
    for one in small:
        one.start()

    barrier = pltpu.get_barrier_semaphore()

    def arrive(target):
        pl.semaphore_signal(barrier, inc=1, device_id=target, device_id_type=MESH)

    for dz in (1, -1, 2, -2):
        arrive(device(x, lo, core, h, z_off(dz)))
    for dx in (1, 2, 3):
        arrive(device(x_off(dx), lo, core, h, z))
    arrive(sibling)
    arrive(partner)
    for g in range(2):

        @pl.when(jnp.logical_not(l_source[g]))
        def _():
            arrive(device(x, lo, core, g, 7 * g))

    for row in range(2):

        @pl.when(jnp.logical_not(root & (h == row)))
        def _():
            arrive(device(3 * core, core, core, row, z))

    for one in small:
        one.wait()

    @pl.when(any_source | root)
    def _():
        pltpu.make_async_copy(data_hbm, data, data_sem).wait()

    def turn(block_rows, store):
        @pl.loop(0, BLK, unroll=2)
        def _(s):
            turned[pl.ds(s, LANES, stride=BLK), :] = block_rows(s).T

        @pl.loop(0, 2 * HALF, unroll=4)
        def _(f):
            store(f, turned[pl.ds(f * BLK, BLK), :].astype(jnp.bfloat16))

    for g in range(2):

        @pl.when(l_source[g])
        def _():
            trace = lax.broadcasted_iota(jnp.int32, (BLK, PANEL), 0) + g * (512 - PANEL)
            scale = jnp.zeros((BLK, 1), jnp.float32)
            for t in range(STEPS):
                found = trace == panel_index[t : t + 1, :]
                scale = scale + jnp.sum(
                    jnp.where(found, panel_weight[t : t + 1, :], 0.0),
                    axis=1,
                    keepdims=True,
                )
            scale = jnp.broadcast_to(scale, (BLK, LANES))

            def block_rows(s):
                parts = []
                for fh in range(2):
                    for c in range(2):
                        part = data[c, s, :, fh * LANES : (fh + 1) * LANES]
                        part = (part.astype(jnp.float32) * scale).astype(jnp.bfloat16)
                        parts.append(part.astype(jnp.float32))
                return jnp.concatenate(parts, axis=0)

            def store(f, value):
                left[g, f // HALF, (f // BLK) % 2, (f // CH) % 8, f % CH] = value

            turn(block_rows, store)

    @pl.when(root)
    def _():
        def block_rows(q):
            return jnp.concatenate(
                [
                    data[c, q, :, fh * LANES : (fh + 1) * LANES].astype(jnp.float32)
                    for c in range(2)
                    for fh in range(2)
                ],
                axis=0,
            )

        def store(f, value):
            right[core, 0, f // HALF, (f // BLK) % 2, (f // 8) % 4, f % 8] = value

        turn(block_rows, store)

    incoming = 9 + 15 * (
        any_source.astype(jnp.int32) + root.astype(jnp.int32)
    )
    pl.semaphore_wait(barrier, incoming)

    def copy(src, dst, send, recv, target):
        return pltpu.make_async_remote_copy(
            src_ref=src, dst_ref=dst, send_sem=send, recv_sem=recv,
            device_id=target, device_id_type=MESH,
        )

    def first_left(g, row, p, u):
        ref = left.at[g, row, u, p]
        return copy(
            ref, ref, l_first.at[row, p, u], l_recv.at[g, p, u],
            device(x, lo, core, row, p),
        )

    def left_copy(g, p, u, slot, to_z):
        ref = left.at[g, h, u, p]
        return copy(
            ref, ref, l_send.at[g, u, slot], l_recv.at[g, p, u],
            device(x, lo, core, h, to_z),
        )

    def left_sends(g, u, level):
        if level == 1:
            return [(z, i, z_off(dz)) for i, dz in enumerate((2, -2, 1, -1))]
        return [
            (z_off(2), 4, z_off(-1)),
            (z_off(-2), 5, z_off(1)),
            (z_off(-2), 6, z_off(2)) if u == 0 else (z_off(2), 6, z_off(-2)),
        ]

    def send_left(g, u, level, wait=False):
        for p, slot, to_z in left_sends(g, u, level):

            @pl.when(jnp.logical_not((h == g) & (to_z == 7 * g)))
            def _():
                one = left_copy(g, p, u, slot, to_z)
                if wait:
                    one.wait_send()
                else:
                    one.start()

    def await_left(g, p, u):
        @pl.when(jnp.logical_not(l_source[g]))
        def _():
            left_copy(g, p, u, 0, z_off(1)).wait_recv()

    def first_right(row, part, to_lo, u):
        rel = jnp.where(row == h, 0, 1)
        return copy(
            right.at[core, 0, row, u, part], right.at[core, rel, row, u, part],
            r_first.at[row, part, to_lo, u], r_recv.at[core, rel, part, u],
            device(part, to_lo, core, row, z),
        )

    def right_copy(g, rel, part, u, send, target):
        ref = right.at[g, rel, h, u, part]
        return copy(ref, ref, send, r_recv.at[g, rel, part, u], target)

    def across_right(rel, u, dx):
        return right_copy(
            core, rel, x, u, r_send.at[rel, u, dx], device(x_off(dx), lo, core, h, z)
        )

    def across_allowed(rel, dx):
        to_root = (x_off(dx) == 3 * core) & (lo == core)
        return jnp.logical_not(to_root) if rel == 0 else to_root | True

    def side_right(rel, part, u):
        return right_copy(core, rel, part, u, r_side.at[rel, part, u], sibling)

    def await_right(rel, part, u):
        def wait():
            right_copy(core, rel, part, u, r_side.at[0, 0, 0], sibling).wait_recv()

        if rel == 0:
            pl.when(jnp.logical_not(root))(wait)
        else:
            wait()

    def spec_copy(p, u):
        return copy(
            spec_out.at[u, p], spec_in.at[u, p], s_send.at[u, p], s_recv.at[u, p], partner
        )

    def scatter(u, wait=False):
        def act(one):
            if wait:
                one.wait_send()
            else:
                one.start()

        for g in range(2):

            @pl.when(l_source[g])
            def _():
                @pl.loop(0, 8)
                def _(i):
                    p = (z + i) % 8
                    act(first_left(g, other, p, u))

                    @pl.when(i > 0)
                    def _():
                        act(first_left(g, h, p, u))

        @pl.when(root)
        def _():
            @pl.loop(0, 4)
            def _(i):
                part = (x + i) % 4
                for to_lo in range(2):
                    act(first_right(other, part, to_lo, u))

                    @pl.when(jnp.logical_not((i == 0) & (lo == to_lo)))
                    def _():
                        act(first_right(h, part, to_lo, u))

    for u in range(2):
        scatter(u)

    fill_table(band, table)

    for u in range(2):
        for g in range(2):
            await_left(g, z, u)
            send_left(g, u, 1)
        for rel in range(2):
            await_right(rel, x, u)
            for dx in (2, 1, 3):

                @pl.when(across_allowed(rel, dx))
                def _():
                    across_right(rel, u, dx).start()

            side_right(rel, x, u).start()

    def pass_left_on(u):
        for g in range(2):
            await_left(g, z_off(2), u)
            await_left(g, z_off(-2), u)
            send_left(g, u, 2)

    def pass_right_on(u):
        for dx in (1, 3, 2):
            for rel in range(2):
                await_right(rel, x_off(dx), u)
                side_right(rel, x_off(dx), u).start()

    def await_side(u):
        for rel in range(2):
            for part in range(4):
                right_copy(
                    1 - core, rel, part, u, r_side.at[0, 0, 0], sibling
                ).wait_recv()

    lane = lax.broadcasted_iota(jnp.int32, (BLK, LANES), 1)
    in_half = [(lane // BLK) % 2 == fh for fh in range(2)]
    keep = [jnp.where(m, 1.0, 0.0).astype(jnp.bfloat16) for m in in_half]
    sign = [
        jnp.where(m, jnp.where(lane < HALF, -1.0, 1.0), 0.0).astype(jnp.bfloat16)
        for m in in_half
    ]

    def spectra(u, begin, end):
        @pl.loop(begin, end)
        def _(n):
            step = (n + 1) // 2
            p = (z + jnp.where(n % 2 == 1, step, 8 - step)) % 8

            @pl.when((n != 0) & (n != 3) & (n != 4))
            def _():
                for g in range(2):
                    await_left(g, p, u)

            for i in range(CH):
                f = h * HALF + u * BLK + p * CH + i
                rows = jnp.concatenate(
                    [left[0, h, u, p, i], left[1, h, u, p, i]], axis=1
                )
                columns = []
                for rel in range(2):
                    parts = []
                    for g in range(2):
                        held = right[g, rel, h, u, p // 2, (p % 2) * CH + i]
                        swapped = jnp.concatenate(
                            [held[:, HALF:], held[:, :HALF]], axis=1
                        )
                        for fh in range(2):
                            parts += [held * keep[fh], swapped * sign[fh]]
                    columns.append(jnp.concatenate(parts, axis=0))
                product = jnp.dot(
                    rows,
                    jnp.concatenate(columns, axis=1),
                    preferred_element_type=jnp.float32,
                )
                z_out[pl.ds(f, BLK, stride=LANES), :] = product[:, :LANES]
                spec_out[u, p, i] = product[:, LANES:].astype(jnp.bfloat16)

            spec_copy(p, u).start()

    def take_in(u):
        @pl.loop(0, 8)
        def _(n):
            step = (n + 1) // 2
            p = (z + jnp.where(n % 2 == 1, step, 8 - step)) % 8
            spec_copy(p, u).wait_recv()
            for i in range(CH):
                f = other * HALF + u * BLK + p * CH + i
                z_out[pl.ds(f, BLK, stride=LANES), :] = spec_in[u, p, i].astype(
                    jnp.float32
                )

    pass_left_on(0)
    pass_right_on(0)
    await_side(0)
    spectra(0, 0, 5)
    pass_left_on(1)
    spectra(0, 5, 8)
    pass_right_on(1)
    await_side(1)
    spectra(1, 0, 8)
    take_in(0)
    take_in(1)

    for u in range(2):
        scatter(u, wait=True)
        for g in range(2):
            send_left(g, u, 1, wait=True)
            send_left(g, u, 2, wait=True)
        for rel in range(2):
            for dx in (1, 2, 3):

                @pl.when(across_allowed(rel, dx))
                def _():
                    across_right(rel, u, dx).wait_send()

            for part in range(4):
                side_right(rel, part, u).wait_send()

        @pl.loop(0, 8)
        def _(p):
            spec_copy(p, u).wait_send()


def fill_table(band, table):
    turns = jnp.float32(2.0 * math.pi / NT)
    bins = jnp.broadcast_to(band[...], (LANES, NF)).T
    sample = lax.broadcasted_iota(jnp.int32, (NF, LANES), 1)
    fine = ((bins * sample) & (NT - 1)).astype(jnp.float32) * turns
    cos_fine, sin_fine = jnp.cos(fine), jnp.sin(fine)
    root_half = jnp.float32(math.sqrt(0.5))
    for block in range(NT // LANES):
        eighth = (bins * block) & 7
        cos_coarse = eighth_cosine(eighth, root_half)
        sin_coarse = eighth_cosine((eighth + 6) & 7, root_half)
        at = slice(block * LANES, (block + 1) * LANES)
        table[:NF, at] = (cos_coarse * cos_fine - sin_coarse * sin_fine).astype(
            jnp.bfloat16
        )
        table[NF:, at] = (-(sin_coarse * cos_fine + cos_coarse * sin_fine)).astype(
            jnp.bfloat16
        )


def eighth_cosine(eighth, root_half):
    size = jnp.where(
        eighth % 2 == 1, root_half, jnp.where(eighth % 4 == 0, 1.0, 0.0)
    )
    return jnp.where((eighth >= 3) & (eighth <= 5), -size, size)


def gathered_spectra(data, panel_index, panel_weight, band):
    vmem = pl.BlockSpec(memory_space=pltpu.VMEM)
    dma = pltpu.SemaphoreType.DMA
    bf16 = jnp.bfloat16
    return pl.pallas_call(
        gather_kernel,
        out_shape=(
            jax.ShapeDtypeStruct((BLK * LANES, LANES), jnp.float32),
            jax.ShapeDtypeStruct((2 * NF, NT), bf16),
        ),
        in_specs=[pl.BlockSpec(memory_space=pltpu.HBM)] * 4,
        out_specs=(vmem, vmem),
        scratch_shapes=[
            pltpu.VMEM((2, BLK, BLK, NF), bf16),
            pltpu.VMEM((STEPS, PANEL), jnp.int32),
            pltpu.VMEM((STEPS, PANEL), jnp.float32),
            pltpu.VMEM((1, NF), jnp.int32),
            pltpu.VMEM((LANES * BLK, LANES), jnp.float32),
            pltpu.VMEM((2, 2, 2, 8, CH, BLK, LANES), bf16),
            pltpu.VMEM((2, 2, 2, 2, 4, 8, BLK, LANES), bf16),
            pltpu.VMEM((2, 8, CH, BLK, LANES), bf16),
            pltpu.VMEM((2, 8, CH, BLK, LANES), bf16),
            dma,
            dma((3,)),
            dma((2, 8, 2)),
            dma((2, 8, 2)),
            dma((2, 2, 7)),
            dma((2, 2, 4, 2)),
            dma((2, 4, 2, 2)),
            dma((2, 2, 4)),
            dma((2, 4, 2)),
            dma((2, 8)),
            dma((2, 8)),
        ],
        compiler_params=pltpu.CompilerParams(
            collective_id=0, has_side_effects=True, vmem_limit_bytes=40 * 2**20
        ),
        cost_estimate=pl.CostEstimate(
            flops=2 * HALF * BLK * 256 * 256,
            bytes_accessed=6 * 2**20,
            transcendentals=2 * NF * LANES,
        ),
        name="gathered_spectra",
    )(data, panel_index, panel_weight, band)


ROWS_AT_ONCE = 8


def to_time_kernel(scale, z_ref, table, out):
    rows = []
    for s in range(ROWS_AT_ONCE):
        turned = z_ref[s * LANES : (s + 1) * LANES, :].T.astype(jnp.bfloat16)
        rows.append(
            jnp.concatenate(
                [turned[j * BLK : (j + 1) * BLK, :] for j in range(4)], axis=1
            )
        )
    product = jnp.dot(
        jnp.concatenate(rows, axis=0), table[...], preferred_element_type=jnp.float32
    )
    out[...] = (product * scale).astype(jnp.bfloat16).reshape(ROWS_AT_ONCE, BLK, NT)


def to_time(z, table, scale):
    steps = BLK // ROWS_AT_ONCE
    return pl.pallas_call(
        functools.partial(to_time_kernel, scale),
        out_shape=jax.ShapeDtypeStruct((BLK, BLK, NT), jnp.bfloat16),
        grid=(steps,),
        in_specs=[
            pl.BlockSpec((ROWS_AT_ONCE * LANES, LANES), lambda i: (i, 0)),
            pl.BlockSpec((2 * NF, NT), lambda i: (0, 0)),
        ],
        out_specs=pl.BlockSpec((ROWS_AT_ONCE, BLK, NT), lambda i: (i, 0, 0)),
        compiler_params=pltpu.CompilerParams(vmem_limit_bytes=40 * 2**20),
        cost_estimate=pl.CostEstimate(
            flops=2 * 1024 * 512 * 1024, bytes_accessed=5 * 2**20, transcendentals=0
        ),
        name="to_time",
    )(z, table)


def body(data, panel_index, panel_weight, band_index):
    z, table = gathered_spectra(
        data, panel_index, panel_weight, band_index.reshape(1, NF)
    )
    norm_scale = 1.0 / math.sqrt(2.0 * STEPS * PANEL * NF)
    return to_time(z, table, -norm_scale)


def solution(mesh):
    placed = (P(None, "src", "rcv", None), P(), P(), P())
    return jax.shard_map(
        body, mesh=mesh, in_specs=placed, out_specs=P("src", "rcv", None), check_vma=False
    )
```

```python
import functools
import math

import jax
import jax.numpy as jnp
from jax import lax
from jax.experimental import pallas as pl
from jax.experimental.pallas import tpu as pltpu
from jax.sharding import PartitionSpec as P

NF = 256
NT = 1024
PANEL = 32
STEPS = 2
BLK = 32
LANES = 128
HALF = 64
CH = 2
NU = 4
PER = HALF // NU
ROWS_AT_ONCE = 8
PARTS = 4
MESH = pl.DeviceIdType.MESH


def device(x, lo, core, h, z):
    return (x * 4 + lo * 2 + core, h * 8 + z)


def here():
    src = lax.axis_index("src")
    rcv = lax.axis_index("rcv")
    return src // 4, (src // 2) % 2, src % 2, rcv // 8, rcv % 8


def gather_kernel(
    data_hbm, small, z_out, table,
    data, turned, left, right, spec_out, spec_in,
    data_sem, l_own, l_past, l_first, l_send,
    r_own, r_rest, r_first, r_send, r_side_send, r_side, s_send, s_recv,
):
    x, lo, core, h, z = here()
    other = 1 - h
    partner = device(x, lo, core, other, z)
    sibling = device(x, lo, 1 - core, h, z)
    beside = device(x, 1 - lo, core, h, z)
    l_source = [(h == g) & (z == 7 * g) for g in range(2)]
    root = (x == 3 * core) & (lo == core)
    any_source = l_source[0] | l_source[1]

    def z_off(dz):
        return (z + dz + 8) % 8

    def x_off(dx):
        return (x + dx) % 4

    @pl.when(any_source | root)
    def _():
        pltpu.make_async_copy(data_hbm, data, data_sem).start()

    barrier = pltpu.get_barrier_semaphore()

    def arrive(target):
        pl.semaphore_signal(barrier, inc=1, device_id=target, device_id_type=MESH)

    for dz in (1, -1, 2, -2):
        arrive(device(x, lo, core, h, z_off(dz)))
    for dx in (1, 2, 3):
        arrive(device(x_off(dx), lo, core, h, z))
    arrive(sibling)
    arrive(partner)
    for g in range(2):

        @pl.when(jnp.logical_not(l_source[g]))
        def _():
            arrive(device(x, lo, core, g, 7 * g))

    for row in range(2):

        @pl.when((lo == core) & jnp.logical_not(root & (h == row)))
        def _():
            arrive(device(3 * core, core, core, row, z))

    @pl.when(lo != core)
    def _():
        arrive(beside)

    @pl.when(any_source | root)
    def _():
        pltpu.make_async_copy(data_hbm, data, data_sem).wait()

    def turn(block_rows, store):
        @pl.loop(0, BLK, unroll=2)
        def _(s):
            turned[pl.ds(s, LANES, stride=BLK), :] = block_rows(s).T

        @pl.loop(0, 2 * HALF, unroll=4)
        def _(f):
            store(f, turned[pl.ds(f * BLK, BLK), :].astype(jnp.bfloat16))

    for g in range(2):

        @pl.when(l_source[g])
        def _():
            trace = lax.broadcasted_iota(jnp.int32, (BLK, STEPS * PANEL), 0)
            trace = trace + g * (512 - PANEL)
            found = trace.astype(jnp.float32) == small[:, : STEPS * PANEL]
            scale = jnp.sum(
                jnp.where(found, small[:, STEPS * PANEL : LANES], 0.0),
                axis=1,
                keepdims=True,
            )
            scale = jnp.broadcast_to(scale, (BLK, LANES))

            def block_rows(s):
                parts = []
                for fh in range(2):
                    for c in range(2):
                        part = data[c, s, :, fh * LANES : (fh + 1) * LANES]
                        part = (part.astype(jnp.float32) * scale).astype(jnp.bfloat16)
                        parts.append(part.astype(jnp.float32))
                return jnp.concatenate(parts, axis=0)

            def store(f, value):
                left[g, f // HALF, (f // PER) % NU, (f // CH) % 8, f % CH] = value

            turn(block_rows, store)

    def turn_right():
        def block_rows(q):
            return jnp.concatenate(
                [
                    data[c, q, :, fh * LANES : (fh + 1) * LANES].astype(jnp.float32)
                    for c in range(2)
                    for fh in range(2)
                ],
                axis=0,
            )

        def store(f, value):
            right[core, 0, f // HALF, (f // PER) % NU, (f // (2 * CH)) % 4, f % (2 * CH)] = value

        turn(block_rows, store)

    pl.when(root & jnp.logical_not(any_source))(turn_right)

    incoming = (
        9
        + 15 * any_source.astype(jnp.int32)
        + 7 * root.astype(jnp.int32)
        + (lo == core).astype(jnp.int32)
    )
    pl.semaphore_wait(barrier, incoming)

    def copy(src, dst, send, recv, target):
        return pltpu.make_async_remote_copy(
            src_ref=src, dst_ref=dst, send_sem=send, recv_sem=recv,
            device_id=target, device_id_type=MESH,
        )

    def await_bytes(ref, sem):
        copy(ref, ref, sem, sem, partner).wait_recv()

    def first_left(g, row, p, u):
        ref = left.at[g, row, u, p]
        sem = l_first.at[jnp.where(row == h, 1, 0)]
        return copy(ref, ref, sem, l_own.at[g, u], device(x, lo, core, row, p))

    def left_sends(g, u, level):
        near, far = l_send.at[g, 0], l_send.at[g, 1]
        if level < 3:
            return [
                (z_off(-level), near, z_off(1)),
                (z_off(level), near, z_off(-1)),
            ]
        way = 1 if u % 2 == 0 else -1
        return [(z_off(-3 * way), far, z_off(way))]

    def send_left(g, u, level):
        for p, send, to_z in left_sends(g, u, level):

            @pl.when(jnp.logical_not((h == g) & (to_z == 7 * g)))
            def _():
                ref = left.at[g, h, u, p]
                recv = l_past.at[level, g, u]
                copy(ref, ref, send, recv, device(x, lo, core, h, to_z)).start()

    def await_left(g, u, count, sem):
        @pl.when(jnp.logical_not(l_source[g]))
        def _():
            await_bytes(left.at[g, h, u, pl.ds(0, count)], sem)

    def left_sent(g):
        beside_source = (h == g) & (z_off(1) == 7 * g)
        beside_source |= (h == g) & (z_off(-1) == 7 * g)
        for is_so, near, rounds in (
            (beside_source, 3, NU // 2),
            (jnp.logical_not(beside_source), 6, NU),
        ):

            @pl.when(is_so)
            def _():
                await_bytes(left.at[g, h, :, pl.ds(0, near)], l_send.at[g, 0])
                await_bytes(left.at[g, h, pl.ds(0, rounds), 0], l_send.at[g, 1])

    def first_right(row, part, u):
        rel = jnp.where(row == h, 0, 1)
        return copy(
            right.at[core, 0, row, u, part], right.at[core, rel, row, u, part],
            r_first.at[1 - rel], r_own.at[rel, u], device(part, lo, core, row, z),
        )

    def right_copy(rel, part, u, send, recv, target):
        ref = right.at[core, rel, h, u, part]
        return copy(ref, ref, send, recv, target)

    def across_right(rel, u, dx):
        return right_copy(
            rel, x, u, r_send.at[rel], r_rest.at[rel, u],
            device(x_off(dx), lo, core, h, z),
        )

    def beside_right(rel, u):
        return right_copy(rel, x, u, r_send.at[2], r_own.at[rel, u], beside)

    def across_allowed(rel, dx):
        to_root = (x_off(dx) == 3 * core) & (lo == core)
        return jnp.logical_not(to_root) if rel == 0 else to_root | True

    def side_right(rel, part, u):
        return right_copy(rel, part, u, r_side_send, r_side.at[u], sibling)

    def await_right(rel, u, count, sem):
        def wait():
            await_bytes(right.at[core, rel, h, u, pl.ds(0, count)], sem.at[rel, u])

        if rel == 0:
            pl.when(jnp.logical_not(root))(wait)
        else:
            wait()

    def spec_copy(p, u):
        return copy(
            spec_out.at[u, p], spec_in.at[u, p], s_send, s_recv.at[u], partner
        )

    def scatter_left(u):
        for g in range(2):

            @pl.when(l_source[g])
            def _():
                @pl.loop(0, 8)
                def _(i):
                    p = (z + i) % 8
                    first_left(g, other, p, u).start()

                    @pl.when(i > 0)
                    def _():
                        first_left(g, h, p, u).start()

    def scatter_right(u):
        @pl.when(root)
        def _():
            @pl.loop(0, 4)
            def _(i):
                part = (x + i) % 4
                first_right(other, part, u).start()

                @pl.when(i > 0)
                def _():
                    first_right(h, part, u).start()

    for u in range(NU):
        scatter_left(u)
    pl.when(root & any_source)(turn_right)
    for u in range(NU):
        scatter_right(u)

    fill_table(small, table)

    def begin_left(u):
        for g in range(2):
            await_left(g, u, 1, l_own.at[g, u])
            send_left(g, u, 0)

    def begin_right(u):
        for rel in range(2):
            await_right(rel, u, 1, r_own)

            @pl.when(lo == core)
            def _():
                beside_right(rel, u).start()

            for dx in (2, 1, 3):

                @pl.when(across_allowed(rel, dx))
                def _():
                    across_right(rel, u, dx).start()

            side_right(rel, x, u).start()

    def pass_left_on(u, level):
        for g in range(2):
            await_left(g, u, 2, l_past.at[level - 1, g, u])
            send_left(g, u, level)

    def pass_right_on(u):
        for rel in range(2):
            await_right(rel, u, 3, r_rest)
            for dx in (1, 2, 3):
                side_right(rel, x_off(dx), u).start()

    def await_side(u):
        await_bytes(right.at[1 - core, :, h, u], r_side.at[u])

    lane = lax.broadcasted_iota(jnp.int32, (BLK, LANES), 1)
    in_half = [(lane // BLK) % 2 == fh for fh in range(2)]
    keep = [jnp.where(m, 1.0, 0.0).astype(jnp.bfloat16) for m in in_half]
    sign = [
        jnp.where(m, jnp.where(lane < HALF, -1.0, 1.0), 0.0).astype(jnp.bfloat16)
        for m in in_half
    ]

    def spectra(u):
        @pl.loop(0, 8)
        def _(p):

            for i in range(CH):
                f = h * HALF + u * PER + p * CH + i
                rows = jnp.concatenate(
                    [left[0, h, u, p, i], left[1, h, u, p, i]], axis=1
                )
                columns = []
                for rel in range(2):
                    parts = []
                    for g in range(2):
                        held = right[g, rel, h, u, p // 2, (p % 2) * CH + i]
                        swapped = jnp.concatenate(
                            [held[:, HALF:], held[:, :HALF]], axis=1
                        )
                        for fh in range(2):
                            parts += [held * keep[fh], swapped * sign[fh]]
                    columns.append(jnp.concatenate(parts, axis=0))
                product = jnp.dot(
                    rows,
                    jnp.concatenate(columns, axis=1),
                    preferred_element_type=jnp.float32,
                )
                z_out[pl.ds(f, BLK, stride=LANES), :] = product[:, :LANES]
                spec_out[u, p, i] = product[:, LANES:].astype(jnp.bfloat16)

            spec_copy(p, u).start()

    def take_in(u):
        await_bytes(spec_in.at[u], s_recv.at[u])

        @pl.loop(0, 8)
        def _(p):
            for i in range(CH):
                f = other * HALF + u * PER + p * CH + i
                z_out[pl.ds(f, BLK, stride=LANES), :] = spec_in[u, p, i].astype(
                    jnp.float32
                )

    def multiply(u):
        for g in range(2):
            await_left(g, u, 1, l_past.at[3, g, u])
        await_side(u)
        spectra(u)

    begin_left(0)
    begin_right(0)
    begin_left(1)
    begin_right(1)
    begin_left(2)
    pass_left_on(0, 1)
    begin_right(2)
    begin_left(3)
    pass_left_on(1, 1)
    begin_right(3)
    pass_left_on(2, 1)
    pass_left_on(0, 2)
    pass_right_on(0)
    pass_left_on(3, 1)
    pass_left_on(1, 2)
    pass_right_on(1)
    pass_left_on(2, 2)
    pass_left_on(0, 3)
    pass_left_on(3, 2)
    pass_left_on(1, 3)
    pass_right_on(2)
    pass_left_on(2, 3)
    multiply(0)
    pass_right_on(3)
    pass_left_on(3, 3)
    multiply(1)
    multiply(2)
    multiply(3)
    for u in range(NU):
        take_in(u)

    for g in range(2):

        @pl.when(l_source[g])
        def _():
            await_bytes(left.at[g, other], l_first.at[0])
            await_bytes(left.at[g, h, :, pl.ds(0, 7)], l_first.at[1])

        left_sent(g)

    @pl.when(root)
    def _():
        await_bytes(right.at[core, 0, other], r_first.at[0])
        await_bytes(right.at[core, 0, h, :, pl.ds(0, 3)], r_first.at[1])

    near_root = (lo == core) & jnp.logical_not(root)
    await_bytes(right.at[core, 1, h, :, pl.ds(0, 3)], r_send.at[1])

    @pl.when(near_root)
    def _():
        await_bytes(right.at[core, 0, h, :, pl.ds(0, 2)], r_send.at[0])

    @pl.when(jnp.logical_not(near_root))
    def _():
        await_bytes(right.at[core, 0, h, :, pl.ds(0, 3)], r_send.at[0])

    @pl.when(lo == core)
    def _():
        await_bytes(right.at[core, :, h, :, 0], r_send.at[2])

    await_bytes(right.at[core, :, h], r_side_send)
    await_bytes(spec_out, s_send)


def fill_table(small, table):
    turns = jnp.float32(2.0 * math.pi / NT)
    bins = jnp.broadcast_to(small[:, LANES:], (LANES, NF)).T.astype(jnp.int32)
    sample = lax.broadcasted_iota(jnp.int32, (NF, LANES), 1)
    fine = ((bins * sample) & (NT - 1)).astype(jnp.float32) * turns
    cos_fine, sin_fine = jnp.cos(fine), jnp.sin(fine)
    root_half = jnp.float32(math.sqrt(0.5))
    for block in range(NT // LANES):
        eighth = (bins * block) & 7
        cos_coarse = eighth_cosine(eighth, root_half)
        sin_coarse = eighth_cosine((eighth + 6) & 7, root_half)
        at = slice(block * LANES, (block + 1) * LANES)
        table[:NF, at] = (cos_coarse * cos_fine - sin_coarse * sin_fine).astype(
            jnp.bfloat16
        )
        table[NF:, at] = (-(sin_coarse * cos_fine + cos_coarse * sin_fine)).astype(
            jnp.bfloat16
        )


def eighth_cosine(eighth, root_half):
    size = jnp.where(
        eighth % 2 == 1, root_half, jnp.where(eighth % 4 == 0, 1.0, 0.0)
    )
    return jnp.where((eighth >= 3) & (eighth <= 5), -size, size)


def gathered_spectra(data, small):
    vmem = pl.BlockSpec(memory_space=pltpu.VMEM)
    dma = pltpu.SemaphoreType.DMA
    bf16 = jnp.bfloat16
    return pl.pallas_call(
        gather_kernel,
        out_shape=(
            jax.ShapeDtypeStruct((BLK * LANES, LANES), jnp.float32),
            jax.ShapeDtypeStruct((2 * NF, NT), bf16),
        ),
        in_specs=[pl.BlockSpec(memory_space=pl.ANY), vmem],
        out_specs=(vmem, vmem),
        scratch_shapes=[
            pltpu.VMEM((2, BLK, BLK, NF), bf16),
            pltpu.VMEM((LANES * BLK, LANES), jnp.float32),
            pltpu.VMEM((2, 2, NU, 8, CH, BLK, LANES), bf16),
            pltpu.VMEM((2, 2, 2, NU, PARTS, 2 * CH, BLK, LANES), bf16),
            pltpu.VMEM((NU, 8, CH, BLK, LANES), bf16),
            pltpu.VMEM((NU, 8, CH, BLK, LANES), bf16),
            dma,
            dma((2, NU)),
            dma((4, 2, NU)),
            dma((2,)),
            dma((2, 2)),
            dma((2, NU)),
            dma((2, NU)),
            dma((2,)),
            dma((3,)),
            dma,
            dma((NU,)),
            dma,
            dma((NU,)),
        ],
        compiler_params=pltpu.CompilerParams(
            collective_id=0, has_side_effects=True, vmem_limit_bytes=40 * 2**20
        ),
        cost_estimate=pl.CostEstimate(
            flops=2 * HALF * BLK * 256 * 256,
            bytes_accessed=4 * 2**20,
            transcendentals=2 * NF * LANES,
        ),
        name="gathered_spectra",
    )(data, small)


def to_time_kernel(scale, z_ref, table, out):
    rows = []
    for s in range(ROWS_AT_ONCE):
        turned = z_ref[s * LANES : (s + 1) * LANES, :].T.astype(jnp.bfloat16)
        rows.append(
            jnp.concatenate(
                [turned[j * BLK : (j + 1) * BLK, :] for j in range(4)], axis=1
            )
        )
    product = jnp.dot(
        jnp.concatenate(rows, axis=0), table[...], preferred_element_type=jnp.float32
    )
    out[...] = (product * scale).astype(jnp.bfloat16).reshape(ROWS_AT_ONCE, BLK, NT)


def to_time(z, table, scale):
    steps = BLK // ROWS_AT_ONCE
    return pl.pallas_call(
        functools.partial(to_time_kernel, scale),
        out_shape=jax.ShapeDtypeStruct((BLK, BLK, NT), jnp.bfloat16),
        grid=(steps,),
        in_specs=[
            pl.BlockSpec((ROWS_AT_ONCE * LANES, LANES), lambda i: (i, 0)),
            pl.BlockSpec((2 * NF, NT), lambda i: (0, 0)),
        ],
        out_specs=pl.BlockSpec((ROWS_AT_ONCE, BLK, NT), lambda i: (i, 0, 0)),
        compiler_params=pltpu.CompilerParams(vmem_limit_bytes=40 * 2**20),
        cost_estimate=pl.CostEstimate(
            flops=2 * 1024 * 512 * 1024, bytes_accessed=5 * 2**20, transcendentals=0
        ),
        name="to_time",
    )(z, table)


def body(data, panel_index, panel_weight, band_index):
    norm_scale = 1.0 / math.sqrt(2.0 * STEPS * PANEL * NF)
    small = jnp.concatenate(
        [
            panel_index.astype(jnp.float32).reshape(1, STEPS * PANEL),
            panel_weight.reshape(1, STEPS * PANEL),
            band_index.astype(jnp.float32).reshape(1, NF),
        ],
        axis=1,
    )
    z, table = gathered_spectra(data, small)
    return to_time(z, table, -norm_scale)


def solution(mesh):
    placed = (P(None, "src", "rcv", None), P(), P(), P())
    return jax.shard_map(
        body, mesh=mesh, in_specs=placed, out_specs=P("src", "rcv", None), check_vma=False
    )
```

```python
import functools
import math

import jax
import jax.numpy as jnp
from jax import lax
from jax.experimental import pallas as pl
from jax.experimental.pallas import tpu as pltpu
from jax.sharding import PartitionSpec as P

NF = 256
NT = 1024
PANEL = 32
STEPS = 2
BLK = 32
LANES = 128
HALF = 64
CH = 2
NU = 4
PER = HALF // NU
ROWS_AT_ONCE = 8
PARTS = 4
MESH = pl.DeviceIdType.MESH


def device(x, lo, core, h, z):
    return (x * 4 + lo * 2 + core, h * 8 + z)


def here():
    src = lax.axis_index("src")
    rcv = lax.axis_index("rcv")
    return src // 4, (src // 2) % 2, src % 2, rcv // 8, rcv % 8


def gather_kernel(
    data, panel_index, panel_weight, band, z_out, table,
    turned, left, right, spec_out, spec_in,
    l_own, l_past, l_first, l_send,
    r_own, r_rest, r_first, r_send, r_side_send, r_side, s_send, s_recv,
):
    x, lo, core, h, z = here()
    other = 1 - h
    partner = device(x, lo, core, other, z)
    sibling = device(x, lo, 1 - core, h, z)
    beside = device(x, 1 - lo, core, h, z)
    l_source = [(h == g) & (z == 7 * g) for g in range(2)]
    root = (x == 3 * core) & (lo == core)
    any_source = l_source[0] | l_source[1]

    def z_off(dz):
        return (z + dz + 8) % 8

    def x_off(dx):
        return (x + dx) % 4

    barrier = pltpu.get_barrier_semaphore()

    def arrive(target):
        pl.semaphore_signal(barrier, inc=1, device_id=target, device_id_type=MESH)

    for dz in (1, -1, 2, -2):
        arrive(device(x, lo, core, h, z_off(dz)))
    for dx in (1, 2, 3):
        arrive(device(x_off(dx), lo, core, h, z))
    arrive(sibling)
    arrive(partner)
    for g in range(2):

        @pl.when(jnp.logical_not(l_source[g]))
        def _():
            arrive(device(x, lo, core, g, 7 * g))

    for row in range(2):

        @pl.when((lo == core) & jnp.logical_not(root & (h == row)))
        def _():
            arrive(device(3 * core, core, core, row, z))

    @pl.when(lo != core)
    def _():
        arrive(beside)

    def turn(block_rows, store):
        @pl.loop(0, BLK, unroll=2)
        def _(s):
            turned[pl.ds(s, LANES, stride=BLK), :] = block_rows(s).T

        @pl.loop(0, 2 * HALF, unroll=4)
        def _(f):
            store(f, turned[pl.ds(f * BLK, BLK), :].astype(jnp.bfloat16))

    for g in range(2):

        @pl.when(l_source[g])
        def _():
            trace = lax.broadcasted_iota(jnp.int32, (BLK, PANEL), 0) + g * (512 - PANEL)
            scale = jnp.zeros((BLK, 1), jnp.float32)
            for t in range(STEPS):
                found = trace == panel_index[t : t + 1, :]
                scale = scale + jnp.sum(
                    jnp.where(found, panel_weight[t : t + 1, :], 0.0),
                    axis=1,
                    keepdims=True,
                )
            scale = jnp.broadcast_to(scale, (BLK, LANES))

            def block_rows(s):
                parts = []
                for fh in range(2):
                    for c in range(2):
                        part = data[c, s, :, fh * LANES : (fh + 1) * LANES]
                        part = (part.astype(jnp.float32) * scale).astype(jnp.bfloat16)
                        parts.append(part.astype(jnp.float32))
                return jnp.concatenate(parts, axis=0)

            def store(f, value):
                left[g, f // HALF, (f // PER) % NU, (f // CH) % 8, f % CH] = value

            turn(block_rows, store)

    def turn_right():
        def block_rows(q):
            return jnp.concatenate(
                [
                    data[c, q, :, fh * LANES : (fh + 1) * LANES].astype(jnp.float32)
                    for c in range(2)
                    for fh in range(2)
                ],
                axis=0,
            )

        def store(f, value):
            right[core, 0, f // HALF, (f // PER) % NU, (f // (2 * CH)) % 4, f % (2 * CH)] = value

        turn(block_rows, store)

    pl.when(root & jnp.logical_not(any_source))(turn_right)

    incoming = (
        9
        + 15 * any_source.astype(jnp.int32)
        + 7 * root.astype(jnp.int32)
        + (lo == core).astype(jnp.int32)
    )
    pl.semaphore_wait(barrier, incoming)

    def copy(src, dst, send, recv, target):
        return pltpu.make_async_remote_copy(
            src_ref=src, dst_ref=dst, send_sem=send, recv_sem=recv,
            device_id=target, device_id_type=MESH,
        )

    def await_bytes(ref, sem):
        copy(ref, ref, sem, sem, partner).wait_recv()

    def first_left(g, row, p, u):
        ref = left.at[g, row, u, p]
        sem = l_first.at[jnp.where(row == h, 1, 0)]
        return copy(ref, ref, sem, l_own.at[g, u], device(x, lo, core, row, p))

    def left_sends(g, u, level):
        near, far = l_send.at[g, 0], l_send.at[g, 1]
        if level < 3:
            return [
                (z_off(-level), near, z_off(1)),
                (z_off(level), near, z_off(-1)),
            ]
        way = 1 if u % 2 == 0 else -1
        return [(z_off(-3 * way), far, z_off(way))]

    def send_left(g, u, level):
        for p, send, to_z in left_sends(g, u, level):

            @pl.when(jnp.logical_not((h == g) & (to_z == 7 * g)))
            def _():
                ref = left.at[g, h, u, p]
                recv = l_past.at[level, g, u]
                copy(ref, ref, send, recv, device(x, lo, core, h, to_z)).start()

    def await_left(g, u, count, sem):
        @pl.when(jnp.logical_not(l_source[g]))
        def _():
            await_bytes(left.at[g, h, u, pl.ds(0, count)], sem)

    def left_sent(g):
        beside_source = (h == g) & (z_off(1) == 7 * g)
        beside_source |= (h == g) & (z_off(-1) == 7 * g)
        for is_so, near, rounds in (
            (beside_source, 3, NU // 2),
            (jnp.logical_not(beside_source), 6, NU),
        ):

            @pl.when(is_so)
            def _():
                await_bytes(left.at[g, h, :, pl.ds(0, near)], l_send.at[g, 0])
                await_bytes(left.at[g, h, pl.ds(0, rounds), 0], l_send.at[g, 1])

    def first_right(row, part, u):
        rel = jnp.where(row == h, 0, 1)
        return copy(
            right.at[core, 0, row, u, part], right.at[core, rel, row, u, part],
            r_first.at[1 - rel], r_own.at[rel, u], device(part, lo, core, row, z),
        )

    def right_copy(rel, part, u, send, recv, target):
        ref = right.at[core, rel, h, u, part]
        return copy(ref, ref, send, recv, target)

    def across_right(rel, u, dx):
        return right_copy(
            rel, x, u, r_send.at[rel], r_rest.at[rel, u],
            device(x_off(dx), lo, core, h, z),
        )

    def beside_right(rel, u):
        return right_copy(rel, x, u, r_send.at[2], r_own.at[rel, u], beside)

    def across_allowed(rel, dx):
        to_root = (x_off(dx) == 3 * core) & (lo == core)
        return jnp.logical_not(to_root) if rel == 0 else to_root | True

    def side_right(rel, part, u):
        return right_copy(rel, part, u, r_side_send, r_side.at[u], sibling)

    def await_right(rel, u, count, sem):
        def wait():
            await_bytes(right.at[core, rel, h, u, pl.ds(0, count)], sem.at[rel, u])

        if rel == 0:
            pl.when(jnp.logical_not(root))(wait)
        else:
            wait()

    def spec_copy(p, u):
        return copy(
            spec_out.at[u, p], spec_in.at[u, p], s_send, s_recv.at[u], partner
        )

    def scatter_left(u):
        for g in range(2):

            @pl.when(l_source[g])
            def _():
                @pl.loop(0, 8)
                def _(i):
                    p = (z + i) % 8
                    first_left(g, other, p, u).start()

                    @pl.when(i > 0)
                    def _():
                        first_left(g, h, p, u).start()

    def scatter_right(u):
        @pl.when(root)
        def _():
            @pl.loop(0, 4)
            def _(i):
                part = (x + i) % 4
                first_right(other, part, u).start()

                @pl.when(i > 0)
                def _():
                    first_right(h, part, u).start()

    for u in range(NU):
        scatter_left(u)
    pl.when(root & any_source)(turn_right)
    for u in range(NU):
        scatter_right(u)

    fill_table(band, table)

    def begin_left(u):
        for g in range(2):
            await_left(g, u, 1, l_own.at[g, u])
            send_left(g, u, 0)

    def begin_right(u):
        for rel in range(2):
            await_right(rel, u, 1, r_own)

            @pl.when(lo == core)
            def _():
                beside_right(rel, u).start()

            for dx in (2, 1, 3):

                @pl.when(across_allowed(rel, dx))
                def _():
                    across_right(rel, u, dx).start()

            side_right(rel, x, u).start()

    def pass_left_on(u, level):
        for g in range(2):
            await_left(g, u, 2, l_past.at[level - 1, g, u])
            send_left(g, u, level)

    def pass_right_on(u):
        for rel in range(2):
            await_right(rel, u, 3, r_rest)
            for dx in (1, 2, 3):
                side_right(rel, x_off(dx), u).start()

    def await_side(u):
        await_bytes(right.at[1 - core, :, h, u], r_side.at[u])

    lane = lax.broadcasted_iota(jnp.int32, (BLK, LANES), 1)
    in_half = [(lane // BLK) % 2 == fh for fh in range(2)]
    keep = [jnp.where(m, 1.0, 0.0).astype(jnp.bfloat16) for m in in_half]
    sign = [
        jnp.where(m, jnp.where(lane < HALF, -1.0, 1.0), 0.0).astype(jnp.bfloat16)
        for m in in_half
    ]

    def spectra(u):
        @pl.loop(0, 8)
        def _(p):

            for i in range(CH):
                f = h * HALF + u * PER + p * CH + i
                rows = jnp.concatenate(
                    [left[0, h, u, p, i], left[1, h, u, p, i]], axis=1
                )
                columns = []
                for rel in range(2):
                    parts = []
                    for g in range(2):
                        held = right[g, rel, h, u, p // 2, (p % 2) * CH + i]
                        swapped = jnp.concatenate(
                            [held[:, HALF:], held[:, :HALF]], axis=1
                        )
                        for fh in range(2):
                            parts += [held * keep[fh], swapped * sign[fh]]
                    columns.append(jnp.concatenate(parts, axis=0))
                product = jnp.dot(
                    rows,
                    jnp.concatenate(columns, axis=1),
                    preferred_element_type=jnp.float32,
                )
                z_out[pl.ds(f, BLK, stride=LANES), :] = product[:, :LANES]
                spec_out[u, p, i] = product[:, LANES:].astype(jnp.bfloat16)

            spec_copy(p, u).start()

    def take_in(u):
        await_bytes(spec_in.at[u], s_recv.at[u])

        @pl.loop(0, 8)
        def _(p):
            for i in range(CH):
                f = other * HALF + u * PER + p * CH + i
                z_out[pl.ds(f, BLK, stride=LANES), :] = spec_in[u, p, i].astype(
                    jnp.float32
                )

    def multiply(u):
        for g in range(2):
            await_left(g, u, 1, l_past.at[3, g, u])
        await_side(u)
        spectra(u)

    begin_left(0)
    begin_right(0)
    begin_left(1)
    begin_right(1)
    begin_left(2)
    pass_left_on(0, 1)
    begin_right(2)
    begin_left(3)
    pass_left_on(1, 1)
    begin_right(3)
    pass_left_on(2, 1)
    pass_left_on(0, 2)
    pass_right_on(0)
    pass_left_on(3, 1)
    pass_left_on(1, 2)
    pass_right_on(1)
    pass_left_on(2, 2)
    pass_left_on(0, 3)
    pass_left_on(3, 2)
    pass_left_on(1, 3)
    pass_right_on(2)
    pass_left_on(2, 3)
    multiply(0)
    pass_right_on(3)
    pass_left_on(3, 3)
    multiply(1)
    multiply(2)
    multiply(3)
    for u in range(NU):
        take_in(u)

    for g in range(2):

        @pl.when(l_source[g])
        def _():
            await_bytes(left.at[g, other], l_first.at[0])
            await_bytes(left.at[g, h, :, pl.ds(0, 7)], l_first.at[1])

        left_sent(g)

    @pl.when(root)
    def _():
        await_bytes(right.at[core, 0, other], r_first.at[0])
        await_bytes(right.at[core, 0, h, :, pl.ds(0, 3)], r_first.at[1])

    near_root = (lo == core) & jnp.logical_not(root)
    await_bytes(right.at[core, 1, h, :, pl.ds(0, 3)], r_send.at[1])

    @pl.when(near_root)
    def _():
        await_bytes(right.at[core, 0, h, :, pl.ds(0, 2)], r_send.at[0])

    @pl.when(jnp.logical_not(near_root))
    def _():
        await_bytes(right.at[core, 0, h, :, pl.ds(0, 3)], r_send.at[0])

    @pl.when(lo == core)
    def _():
        await_bytes(right.at[core, :, h, :, 0], r_send.at[2])

    await_bytes(right.at[core, :, h], r_side_send)
    await_bytes(spec_out, s_send)


def fill_table(band, table):
    turns = jnp.float32(2.0 * math.pi / NT)
    bins = jnp.broadcast_to(band[...], (LANES, NF)).T
    sample = lax.broadcasted_iota(jnp.int32, (NF, LANES), 1)
    fine = ((bins * sample) & (NT - 1)).astype(jnp.float32) * turns
    cos_fine, sin_fine = jnp.cos(fine), jnp.sin(fine)
    root_half = jnp.float32(math.sqrt(0.5))
    for block in range(NT // LANES):
        eighth = (bins * block) & 7
        cos_coarse = eighth_cosine(eighth, root_half)
        sin_coarse = eighth_cosine((eighth + 6) & 7, root_half)
        at = slice(block * LANES, (block + 1) * LANES)
        table[:NF, at] = (cos_coarse * cos_fine - sin_coarse * sin_fine).astype(
            jnp.bfloat16
        )
        table[NF:, at] = (-(sin_coarse * cos_fine + cos_coarse * sin_fine)).astype(
            jnp.bfloat16
        )


def eighth_cosine(eighth, root_half):
    size = jnp.where(
        eighth % 2 == 1, root_half, jnp.where(eighth % 4 == 0, 1.0, 0.0)
    )
    return jnp.where((eighth >= 3) & (eighth <= 5), -size, size)


def gathered_spectra(data, panel_index, panel_weight, band):
    vmem = pl.BlockSpec(memory_space=pltpu.VMEM)
    dma = pltpu.SemaphoreType.DMA
    bf16 = jnp.bfloat16
    return pl.pallas_call(
        gather_kernel,
        out_shape=(
            jax.ShapeDtypeStruct((BLK * LANES, LANES), jnp.float32),
            jax.ShapeDtypeStruct((2 * NF, NT), bf16),
        ),
        in_specs=[vmem] * 4,
        out_specs=(vmem, vmem),
        scratch_shapes=[
            pltpu.VMEM((LANES * BLK, LANES), jnp.float32),
            pltpu.VMEM((2, 2, NU, 8, CH, BLK, LANES), bf16),
            pltpu.VMEM((2, 2, 2, NU, PARTS, 2 * CH, BLK, LANES), bf16),
            pltpu.VMEM((NU, 8, CH, BLK, LANES), bf16),
            pltpu.VMEM((NU, 8, CH, BLK, LANES), bf16),
            dma((2, NU)),
            dma((4, 2, NU)),
            dma((2,)),
            dma((2, 2)),
            dma((2, NU)),
            dma((2, NU)),
            dma((2,)),
            dma((3,)),
            dma,
            dma((NU,)),
            dma,
            dma((NU,)),
        ],
        compiler_params=pltpu.CompilerParams(
            collective_id=0, has_side_effects=True, vmem_limit_bytes=40 * 2**20
        ),
        cost_estimate=pl.CostEstimate(
            flops=2 * HALF * BLK * 256 * 256,
            bytes_accessed=4 * 2**20,
            transcendentals=2 * NF * LANES,
        ),
        name="gathered_spectra",
    )(data, panel_index, panel_weight, band)


def to_time_kernel(scale, z_ref, table, out):
    rows = []
    for s in range(ROWS_AT_ONCE):
        turned = z_ref[s * LANES : (s + 1) * LANES, :].T.astype(jnp.bfloat16)
        rows.append(
            jnp.concatenate(
                [turned[j * BLK : (j + 1) * BLK, :] for j in range(4)], axis=1
            )
        )
    product = jnp.dot(
        jnp.concatenate(rows, axis=0), table[...], preferred_element_type=jnp.float32
    )
    out[...] = (product * scale).astype(jnp.bfloat16).reshape(ROWS_AT_ONCE, BLK, NT)


def to_time(z, table, scale):
    steps = BLK // ROWS_AT_ONCE
    return pl.pallas_call(
        functools.partial(to_time_kernel, scale),
        out_shape=jax.ShapeDtypeStruct((BLK, BLK, NT), jnp.bfloat16),
        grid=(steps,),
        in_specs=[
            pl.BlockSpec((ROWS_AT_ONCE * LANES, LANES), lambda i: (i, 0)),
            pl.BlockSpec((2 * NF, NT), lambda i: (0, 0)),
        ],
        out_specs=pl.BlockSpec((ROWS_AT_ONCE, BLK, NT), lambda i: (i, 0, 0)),
        compiler_params=pltpu.CompilerParams(vmem_limit_bytes=40 * 2**20),
        cost_estimate=pl.CostEstimate(
            flops=2 * 1024 * 512 * 1024, bytes_accessed=5 * 2**20, transcendentals=0
        ),
        name="to_time",
    )(z, table)


def body(data, panel_index, panel_weight, band_index):
    norm_scale = 1.0 / math.sqrt(2.0 * STEPS * PANEL * NF)
    z, table = gathered_spectra(
        data, panel_index, panel_weight, band_index.reshape(1, NF)
    )
    return to_time(z, table, -norm_scale)


def solution(mesh):
    placed = (P(None, "src", "rcv", None), P(), P(), P())
    return jax.shard_map(
        body, mesh=mesh, in_specs=placed, out_specs=P("src", "rcv", None), check_vma=False
    )
```

```python
import functools
import math

import jax
import jax.numpy as jnp
from jax import lax
from jax.experimental import pallas as pl
from jax.experimental.pallas import tpu as pltpu
from jax.sharding import PartitionSpec as P

NF = 256
NT = 1024
PANEL = 32
STEPS = 2
BLK = 32
LANES = 128
HALF = 64
CH = 2
NU = 4
PER = HALF // NU
ROWS_AT_ONCE = 16
PARTS = 4
MESH = pl.DeviceIdType.MESH


def device(x, lo, core, h, z):
    return (x * 4 + lo * 2 + core, h * 8 + z)


def here():
    src = lax.axis_index("src")
    rcv = lax.axis_index("rcv")
    return src // 4, (src // 2) % 2, src % 2, rcv // 8, rcv % 8


def gather_kernel(
    data, panel_index, panel_weight, band, z_out, table,
    turned, left, right, spec_out, spec_in,
    l_own, l_past, l_first, l_send,
    r_own, r_rest, r_first, r_send, r_side_send, r_side, s_send, s_recv,
):
    x, lo, core, h, z = here()
    other = 1 - h
    partner = device(x, lo, core, other, z)
    sibling = device(x, lo, 1 - core, h, z)
    beside = device(x, 1 - lo, core, h, z)
    l_source = [(h == g) & (z == 7 * g) for g in range(2)]
    root = (x == 3 * core) & (lo == core)
    any_source = l_source[0] | l_source[1]

    def z_off(dz):
        return (z + dz + 8) % 8

    def x_off(dx):
        return (x + dx) % 4

    barrier = pltpu.get_barrier_semaphore()

    def arrive(target):
        pl.semaphore_signal(barrier, inc=1, device_id=target, device_id_type=MESH)

    for dz in (1, -1, 2, -2):
        arrive(device(x, lo, core, h, z_off(dz)))
    for dx in (1, 2, 3):
        arrive(device(x_off(dx), lo, core, h, z))
    arrive(sibling)
    arrive(partner)
    for g in range(2):

        @pl.when(jnp.logical_not(l_source[g]))
        def _():
            arrive(device(x, lo, core, g, 7 * g))

    for row in range(2):

        @pl.when((lo == core) & jnp.logical_not(root & (h == row)))
        def _():
            arrive(device(3 * core, core, core, row, z))

    @pl.when(lo != core)
    def _():
        arrive(beside)

    def turn(block_rows, store):
        @pl.loop(0, BLK, unroll=8)
        def _(s):
            turned[pl.ds(s, LANES, stride=BLK), :] = block_rows(s).T

        @pl.loop(0, 2 * HALF, unroll=16)
        def _(f):
            store(f, turned[pl.ds(f * BLK, BLK), :].astype(jnp.bfloat16))

    for g in range(2):

        @pl.when(l_source[g])
        def _():
            trace = lax.broadcasted_iota(jnp.int32, (BLK, PANEL), 0) + g * (512 - PANEL)
            scale = jnp.zeros((BLK, 1), jnp.float32)
            for t in range(STEPS):
                found = trace == panel_index[t : t + 1, :]
                scale = scale + jnp.sum(
                    jnp.where(found, panel_weight[t : t + 1, :], 0.0),
                    axis=1,
                    keepdims=True,
                )
            scale = jnp.broadcast_to(scale, (BLK, LANES))

            def block_rows(s):
                parts = []
                for fh in range(2):
                    for c in range(2):
                        part = data[c, s, :, fh * LANES : (fh + 1) * LANES]
                        part = (part.astype(jnp.float32) * scale).astype(jnp.bfloat16)
                        parts.append(part.astype(jnp.float32))
                return jnp.concatenate(parts, axis=0)

            def store(f, value):
                left[g, f // HALF, (f // PER) % NU, (f // CH) % 8, f % CH] = value

            turn(block_rows, store)

    def turn_right():
        def block_rows(q):
            return jnp.concatenate(
                [
                    data[c, q, :, fh * LANES : (fh + 1) * LANES].astype(jnp.float32)
                    for c in range(2)
                    for fh in range(2)
                ],
                axis=0,
            )

        def store(f, value):
            right[core, 0, f // HALF, (f // PER) % NU, (f // (2 * CH)) % 4, f % (2 * CH)] = value

        turn(block_rows, store)

    pl.when(root & jnp.logical_not(any_source))(turn_right)

    incoming = (
        9
        + 15 * any_source.astype(jnp.int32)
        + 7 * root.astype(jnp.int32)
        + (lo == core).astype(jnp.int32)
    )
    pl.semaphore_wait(barrier, incoming)

    def copy(src, dst, send, recv, target):
        return pltpu.make_async_remote_copy(
            src_ref=src, dst_ref=dst, send_sem=send, recv_sem=recv,
            device_id=target, device_id_type=MESH,
        )

    def await_bytes(ref, sem):
        copy(ref, ref, sem, sem, partner).wait_recv()

    def first_left(g, row, p, u):
        ref = left.at[g, row, u, p]
        sem = l_first.at[jnp.where(row == h, 1, 0)]
        return copy(ref, ref, sem, l_own.at[g, u], device(x, lo, core, row, p))

    def left_sends(g, u, level):
        near, far = l_send.at[g, 0], l_send.at[g, 1]
        if level < 3:
            return [
                (z_off(-level), near, z_off(1)),
                (z_off(level), near, z_off(-1)),
            ]
        way = 1 if u % 2 == 0 else -1
        return [(z_off(-3 * way), far, z_off(way))]

    def send_left(g, u, level):
        for p, send, to_z in left_sends(g, u, level):

            @pl.when(jnp.logical_not((h == g) & (to_z == 7 * g)))
            def _():
                ref = left.at[g, h, u, p]
                recv = l_past.at[level, g, u]
                copy(ref, ref, send, recv, device(x, lo, core, h, to_z)).start()

    def await_left(g, u, count, sem):
        @pl.when(jnp.logical_not(l_source[g]))
        def _():
            await_bytes(left.at[g, h, u, pl.ds(0, count)], sem)

    def left_sent(g):
        beside_source = (h == g) & (z_off(1) == 7 * g)
        beside_source |= (h == g) & (z_off(-1) == 7 * g)
        for is_so, near, rounds in (
            (beside_source, 3, NU // 2),
            (jnp.logical_not(beside_source), 6, NU),
        ):

            @pl.when(is_so)
            def _():
                await_bytes(left.at[g, h, :, pl.ds(0, near)], l_send.at[g, 0])
                await_bytes(left.at[g, h, pl.ds(0, rounds), 0], l_send.at[g, 1])

    def first_right(row, part, u):
        rel = jnp.where(row == h, 0, 1)
        return copy(
            right.at[core, 0, row, u, part], right.at[core, rel, row, u, part],
            r_first.at[1 - rel], r_own.at[rel, u], device(part, lo, core, row, z),
        )

    def right_copy(rel, part, u, send, recv, target):
        ref = right.at[core, rel, h, u, part]
        return copy(ref, ref, send, recv, target)

    def across_right(rel, u, dx):
        return right_copy(
            rel, x, u, r_send.at[rel], r_rest.at[rel, u],
            device(x_off(dx), lo, core, h, z),
        )

    def beside_right(rel, u):
        return right_copy(rel, x, u, r_send.at[2], r_own.at[rel, u], beside)

    def across_allowed(rel, dx):
        to_root = (x_off(dx) == 3 * core) & (lo == core)
        return jnp.logical_not(to_root) if rel == 0 else to_root | True

    def side_right(rel, part, u):
        return right_copy(rel, part, u, r_side_send, r_side.at[u], sibling)

    def await_right(rel, u, count, sem):
        def wait():
            await_bytes(right.at[core, rel, h, u, pl.ds(0, count)], sem.at[rel, u])

        if rel == 0:
            pl.when(jnp.logical_not(root))(wait)
        else:
            wait()

    def spec_copy(p, u):
        return copy(
            spec_out.at[u, p], spec_in.at[u, p], s_send, s_recv.at[u], partner
        )

    def scatter_left(u):
        for g in range(2):

            @pl.when(l_source[g])
            def _():
                @pl.loop(0, 8)
                def _(i):
                    p = (z + i) % 8
                    first_left(g, other, p, u).start()

                    @pl.when(i > 0)
                    def _():
                        first_left(g, h, p, u).start()

    def scatter_right(u):
        @pl.when(root)
        def _():
            @pl.loop(0, 4)
            def _(i):
                part = (x + i) % 4
                first_right(other, part, u).start()

                @pl.when(i > 0)
                def _():
                    first_right(h, part, u).start()

    for u in range(NU):
        scatter_left(u)
    pl.when(root & any_source)(turn_right)
    for u in range(NU):
        scatter_right(u)

    fill_table(band, table)

    def begin_left(u):
        for g in range(2):
            await_left(g, u, 1, l_own.at[g, u])
            send_left(g, u, 0)

    def begin_right(u):
        for rel in range(2):
            await_right(rel, u, 1, r_own)

            @pl.when(lo == core)
            def _():
                beside_right(rel, u).start()

            for dx in (2, 1, 3):

                @pl.when(across_allowed(rel, dx))
                def _():
                    across_right(rel, u, dx).start()

            side_right(rel, x, u).start()

    def pass_left_on(u, level):
        for g in range(2):
            await_left(g, u, 2, l_past.at[level - 1, g, u])
            send_left(g, u, level)

    def pass_right_on(u):
        for rel in range(2):
            await_right(rel, u, 3, r_rest)
            for dx in (1, 2, 3):
                side_right(rel, x_off(dx), u).start()

    def await_side(u):
        await_bytes(right.at[1 - core, :, h, u], r_side.at[u])

    lane = lax.broadcasted_iota(jnp.int32, (BLK, LANES), 1)
    in_half = [(lane // BLK) % 2 == fh for fh in range(2)]
    keep = [jnp.where(m, 1.0, 0.0).astype(jnp.bfloat16) for m in in_half]
    sign = [
        jnp.where(m, jnp.where(lane < HALF, -1.0, 1.0), 0.0).astype(jnp.bfloat16)
        for m in in_half
    ]

    def spectra(u):
        @pl.loop(0, 8)
        def _(p):

            for i in range(CH):
                f = h * HALF + u * PER + p * CH + i
                rows = jnp.concatenate(
                    [left[0, h, u, p, i], left[1, h, u, p, i]], axis=1
                )
                columns = []
                for rel in range(2):
                    parts = []
                    for g in range(2):
                        held = right[g, rel, h, u, p // 2, (p % 2) * CH + i]
                        swapped = jnp.concatenate(
                            [held[:, HALF:], held[:, :HALF]], axis=1
                        )
                        for fh in range(2):
                            parts += [held * keep[fh], swapped * sign[fh]]
                    columns.append(jnp.concatenate(parts, axis=0))
                product = jnp.dot(
                    rows,
                    jnp.concatenate(columns, axis=1),
                    preferred_element_type=jnp.float32,
                )
                z_out[pl.ds(f, BLK, stride=LANES), :] = product[:, :LANES]
                spec_out[u, p, i] = product[:, LANES:].astype(jnp.bfloat16)

            spec_copy(p, u).start()

    def take_in(u):
        await_bytes(spec_in.at[u], s_recv.at[u])

        @pl.loop(0, 8)
        def _(p):
            for i in range(CH):
                f = other * HALF + u * PER + p * CH + i
                z_out[pl.ds(f, BLK, stride=LANES), :] = spec_in[u, p, i].astype(
                    jnp.float32
                )

    def multiply(u):
        for g in range(2):
            await_left(g, u, 1, l_past.at[3, g, u])
        await_side(u)
        spectra(u)

    begin_left(0)
    begin_right(0)
    begin_left(1)
    begin_right(1)
    begin_left(2)
    pass_left_on(0, 1)
    begin_right(2)
    begin_left(3)
    pass_left_on(1, 1)
    begin_right(3)
    pass_left_on(0, 2)
    pass_left_on(2, 1)
    pass_right_on(0)
    pass_left_on(1, 2)
    pass_left_on(3, 1)
    pass_left_on(0, 3)
    pass_right_on(1)
    pass_left_on(2, 2)
    pass_left_on(1, 3)
    multiply(0)
    pass_left_on(3, 2)
    pass_right_on(2)
    pass_left_on(2, 3)
    multiply(1)
    pass_right_on(3)
    pass_left_on(3, 3)
    multiply(2)
    multiply(3)
    for u in range(NU):
        take_in(u)

    for g in range(2):

        @pl.when(l_source[g])
        def _():
            await_bytes(left.at[g, other], l_first.at[0])
            await_bytes(left.at[g, h, :, pl.ds(0, 7)], l_first.at[1])

        left_sent(g)

    @pl.when(root)
    def _():
        await_bytes(right.at[core, 0, other], r_first.at[0])
        await_bytes(right.at[core, 0, h, :, pl.ds(0, 3)], r_first.at[1])

    near_root = (lo == core) & jnp.logical_not(root)
    await_bytes(right.at[core, 1, h, :, pl.ds(0, 3)], r_send.at[1])

    @pl.when(near_root)
    def _():
        await_bytes(right.at[core, 0, h, :, pl.ds(0, 2)], r_send.at[0])

    @pl.when(jnp.logical_not(near_root))
    def _():
        await_bytes(right.at[core, 0, h, :, pl.ds(0, 3)], r_send.at[0])

    @pl.when(lo == core)
    def _():
        await_bytes(right.at[core, :, h, :, 0], r_send.at[2])

    await_bytes(right.at[core, :, h], r_side_send)
    await_bytes(spec_out, s_send)


def fill_table(band, table):
    turns = jnp.float32(2.0 * math.pi / NT)
    bins = jnp.broadcast_to(band[...], (LANES, NF)).T
    sample = lax.broadcasted_iota(jnp.int32, (NF, LANES), 1)
    fine = ((bins * sample) & (NT - 1)).astype(jnp.float32) * turns
    cos_fine, sin_fine = jnp.cos(fine), jnp.sin(fine)
    root_half = jnp.float32(math.sqrt(0.5))
    for block in range(NT // LANES):
        eighth = (bins * block) & 7
        cos_coarse = eighth_cosine(eighth, root_half)
        sin_coarse = eighth_cosine((eighth + 6) & 7, root_half)
        at = slice(block * LANES, (block + 1) * LANES)
        table[:NF, at] = (cos_coarse * cos_fine - sin_coarse * sin_fine).astype(
            jnp.bfloat16
        )
        table[NF:, at] = (-(sin_coarse * cos_fine + cos_coarse * sin_fine)).astype(
            jnp.bfloat16
        )


def eighth_cosine(eighth, root_half):
    size = jnp.where(
        eighth % 2 == 1, root_half, jnp.where(eighth % 4 == 0, 1.0, 0.0)
    )
    return jnp.where((eighth >= 3) & (eighth <= 5), -size, size)


def gathered_spectra(data, panel_index, panel_weight, band):
    vmem = pl.BlockSpec(memory_space=pltpu.VMEM)
    dma = pltpu.SemaphoreType.DMA
    bf16 = jnp.bfloat16
    return pl.pallas_call(
        gather_kernel,
        out_shape=(
            jax.ShapeDtypeStruct((BLK * LANES, LANES), jnp.float32),
            jax.ShapeDtypeStruct((2 * NF, NT), bf16),
        ),
        in_specs=[vmem] * 4,
        out_specs=(vmem, vmem),
        scratch_shapes=[
            pltpu.VMEM((LANES * BLK, LANES), jnp.float32),
            pltpu.VMEM((2, 2, NU, 8, CH, BLK, LANES), bf16),
            pltpu.VMEM((2, 2, 2, NU, PARTS, 2 * CH, BLK, LANES), bf16),
            pltpu.VMEM((NU, 8, CH, BLK, LANES), bf16),
            pltpu.VMEM((NU, 8, CH, BLK, LANES), bf16),
            dma((2, NU)),
            dma((4, 2, NU)),
            dma((2,)),
            dma((2, 2)),
            dma((2, NU)),
            dma((2, NU)),
            dma((2,)),
            dma((3,)),
            dma,
            dma((NU,)),
            dma,
            dma((NU,)),
        ],
        compiler_params=pltpu.CompilerParams(
            collective_id=0, has_side_effects=True, vmem_limit_bytes=40 * 2**20
        ),
        cost_estimate=pl.CostEstimate(
            flops=2 * HALF * BLK * 256 * 256,
            bytes_accessed=4 * 2**20,
            transcendentals=2 * NF * LANES,
        ),
        name="gathered_spectra",
    )(data, panel_index, panel_weight, band)


def to_time_kernel(scale, z_ref, table, out):
    rows = []
    for s in range(ROWS_AT_ONCE):
        turned = z_ref[s * LANES : (s + 1) * LANES, :].T.astype(jnp.bfloat16)
        rows.append(
            jnp.concatenate(
                [turned[j * BLK : (j + 1) * BLK, :] for j in range(4)], axis=1
            )
        )
    product = jnp.dot(
        jnp.concatenate(rows, axis=0), table[...], preferred_element_type=jnp.float32
    )
    out[...] = (product * scale).astype(jnp.bfloat16).reshape(ROWS_AT_ONCE, BLK, NT)


def to_time(z, table, scale):
    steps = BLK // ROWS_AT_ONCE
    return pl.pallas_call(
        functools.partial(to_time_kernel, scale),
        out_shape=jax.ShapeDtypeStruct((BLK, BLK, NT), jnp.bfloat16),
        grid=(steps,),
        in_specs=[
            pl.BlockSpec((ROWS_AT_ONCE * LANES, LANES), lambda i: (i, 0)),
            pl.BlockSpec((2 * NF, NT), lambda i: (0, 0)),
        ],
        out_specs=pl.BlockSpec((ROWS_AT_ONCE, BLK, NT), lambda i: (i, 0, 0)),
        compiler_params=pltpu.CompilerParams(vmem_limit_bytes=40 * 2**20),
        cost_estimate=pl.CostEstimate(
            flops=2 * 1024 * 512 * 1024, bytes_accessed=5 * 2**20, transcendentals=0
        ),
        name="to_time",
    )(z, table)


def body(data, panel_index, panel_weight, band_index):
    norm_scale = 1.0 / math.sqrt(2.0 * STEPS * PANEL * NF)
    z, table = gathered_spectra(
        data, panel_index, panel_weight, band_index.reshape(1, NF)
    )
    return to_time(z, table, -norm_scale)


def solution(mesh):
    placed = (P(None, "src", "rcv", None), P(), P(), P())
    return jax.shard_map(
        body, mesh=mesh, in_specs=placed, out_specs=P("src", "rcv", None), check_vma=False
    )
```
